32 devices in a mesh: az: 16 (over z, y, x), grp: 2 (over core).
Axes of the slice: x: 2, y: 2, z: 4, core: 2. Of those that a mesh axis runs over, the one named last changes fastest.
Arguments:
- features: bfloat16 [256, 64, 128], P(None, 'az', 'grp'), may hold values from -6 to 6
- cotangent: bfloat16 [256, 64, 128], P(None, 'az', 'grp'), may hold values from -6 to 6
- w_first: bfloat16 [256, 6912], P('grp'), may hold values from -0.078125 to 0.078125
- w_second: bfloat16 [256, 6912], P('grp'), may hold values from -0.078125 to 0.078125
Outputs:
- flow_out: bfloat16 [256, 64, 128], P(None, 'az', 'grp')
- grad_first: float32 [256, 6912], P('grp')
- grad_second: float32 [256, 6912], P('grp')
The draws below stay inside these ranges and needn't reach their ends.
All inputs are finite; a program needn't handle non-finite values.
Results may differ from the reference program's by a relative error of at most 0.01.
Values may be sent and summed in bfloat16 or wider, within the bound.
No kernel may reach another device: no remote copies, remote signals or barrier semaphores. Data moves between devices by JAX's collectives and lax.ppermute only.
A program may use at most 128 MiB of HBM per device.

```python
import math
import jax
import jax.numpy as jnp
from jax import lax

CH = 256
AZ_DEV = 4
AXIAL = 8
TAPS = 6912
NAZ = 64
NRAD = 16
NRZ = 128
CELLS = 8192
N_AZ = 16


def shard_levels(own_key, extent, split, low, largest):
    factor_of = 1.0
    for position, blocks in split:
        draws = jax.random.uniform(jax.random.fold_in(jax.random.fold_in(own_key, 6), position), (blocks,), jnp.float32, low / len(split), largest / len(split))
        factor_of = factor_of * jnp.repeat(jnp.exp(draws), extent[position] // blocks).reshape((-1,) + (1,) * (len(extent) - 1 - position))
    return factor_of


def bell_draw(rng, shape, spread, most, cuts=(), held_as=jnp.bfloat16):
    level = shard_levels(rng, shape, cuts, -0.22, 0.18) if cuts else 1.0
    drawn = jax.random.normal(rng, shape, jnp.float32) * spread * level
    return jnp.minimum(jnp.maximum(drawn, -most), most).astype(held_as)


def setup_inputs(seed: int = 0) -> dict:
    keys = jax.random.split(jax.random.key(seed), 5)
    features = bell_draw(keys[0], (CH, NAZ, NRZ), 1.0, 6.0, ((1, 16), (2, 2)))
    cotangent = bell_draw(keys[1], (CH, NAZ, NRZ), 1.0, 6.0, ((1, 16), (2, 2)))
    w_first = bell_draw(keys[2], (CH, TAPS), TAPS ** -0.5, 0.078125, ((0, 2),))
    w_second = bell_draw(keys[3], (CH, TAPS), TAPS ** -0.5, 0.078125, ((0, 2),))
    return {"features": features, "cotangent": cotangent, "w_first": w_first, "w_second": w_second}


def silu_slope(values):
    sigma = jax.nn.sigmoid(values)
    return sigma * (1.0 + values * (1.0 - sigma))

def patches(padded, flipped):
    channels, span_az, span_rad, span_ax = padded.shape
    inner_az = span_az - 2
    inner_rad = span_rad - 2
    inner_ax = span_ax - 2
    stacked = []
    for along_az in range(3):
        for along_rad in range(3):
            for along_ax in range(3):
                if flipped:
                    first_az, first_rad, first_ax = (2 - along_az, 2 - along_rad, 2 - along_ax)
                else:
                    first_az, first_rad, first_ax = (along_az, along_rad, along_ax)
                stacked.append(padded[:, first_az:first_az + inner_az, first_rad:first_rad + inner_rad, first_ax:first_ax + inner_ax])
    return jnp.stack(stacked, axis=0).reshape(27 * channels, inner_az * inner_rad * inner_ax)

def pad_full(field):
    looped = jnp.concatenate([field[:, -1:], field, field[:, :1]], axis=1)
    return jnp.pad(looped, ((0, 0), (0, 0), (1, 1), (1, 1)))

def conv_full(padded, weight, flipped):

    def one_block(block):
        window = lax.dynamic_slice_in_dim(padded, block * AZ_DEV, AZ_DEV + 2, 1)
        result = jnp.dot(weight, patches(window, flipped), preferred_element_type=jnp.float32)
        return result.reshape(CH, AZ_DEV, NRZ)
    blocks = lax.map(one_block, jnp.arange(N_AZ, dtype=jnp.int32))
    return blocks.transpose(1, 0, 2, 3).reshape(CH, NAZ, NRZ)

def weight_grad(source, padded):

    def add_block(running, block):
        window = lax.dynamic_slice_in_dim(padded, block * AZ_DEV, AZ_DEV + 2, 1)
        rows_now = lax.dynamic_slice_in_dim(source, block * AZ_DEV, AZ_DEV, 1).reshape(CH, AZ_DEV * NRZ)
        update = lax.dot_general(rows_now, patches(window, False), (((1,), (1,)), ((), ())), preferred_element_type=jnp.float32)
        return (running + update, None)
    running, unused = lax.scan(add_block, jnp.zeros((CH, TAPS), jnp.float32), jnp.arange(N_AZ, dtype=jnp.int32))
    return running

def reference(features, cotangent, w_first, w_second):
    padded_in = pad_full(features.reshape(CH, NAZ, NRAD, AXIAL))
    pre_first = conv_full(padded_in, w_first, False)
    hidden = jax.nn.silu(pre_first).astype(jnp.bfloat16)
    padded_hidden = pad_full(hidden.reshape(CH, NAZ, NRAD, AXIAL))
    second = conv_full(padded_hidden, w_second, False)
    flow_out = (features.astype(jnp.float32) + second).astype(jnp.bfloat16)
    flipped_weight = w_second.reshape(CH, 27, CH).transpose(2, 1, 0).reshape(CH, 27 * CH)
    padded_cot = pad_full(cotangent.reshape(CH, NAZ, NRAD, AXIAL))
    back_grad = conv_full(padded_cot, flipped_weight, True)
    slope = (back_grad * silu_slope(pre_first)).astype(jnp.bfloat16)
    factor = 1.0 / math.sqrt(CELLS)
    grad_second = weight_grad(cotangent, padded_hidden) * factor
    grad_first = weight_grad(slope, padded_in) * factor
    return (flow_out, grad_first, grad_second)
```

```python
import functools
import math

import jax
import jax.numpy as jnp
from jax import lax
from jax.experimental import pallas as pl
from jax.experimental.pallas import tpu as pltpu
from jax.sharding import PartitionSpec as P

AXIAL = 8
NRZ = 128
HALF = 64
LANES = 128
CH = 256
LAYERS = 4
TAPS = 27
BLOCK = 16
FIRST_TAPS = 14
ROWS = TAPS * BLOCK
FIRST = FIRST_TAPS * BLOCK
LAST = ROWS - FIRST
VMEM_LIMIT = 40 * 1024 * 1024
BF16 = jnp.bfloat16
F32 = jnp.float32


def params():
    return pltpu.CompilerParams(vmem_limit_bytes=VMEM_LIMIT)


def vmem():
    return pl.BlockSpec(memory_space=pltpu.VMEM)


def anywhere():
    return pl.BlockSpec(memory_space=pl.ANY)


def smem():
    return pl.BlockSpec(memory_space=pltpu.SMEM)


def shape(dims, kind=BF16):
    return jax.ShapeDtypeStruct(dims, kind)


def cost(flops, moved):
    return pl.CostEstimate(flops=flops, bytes_accessed=moved, transcendentals=0)


def az_extents(count):
    side = 1
    while (2 * side) ** 3 <= count:
        side *= 2
    if count % (side * side):
        side = 1
    return {"z": count // (side * side), "y": side, "x": side}


def az_places(count):
    extents = az_extents(count)
    places = []
    for index in range(count):
        rest, x = divmod(index, extents["x"])
        z, y = divmod(rest, extents["y"])
        places.append({"z": z, "y": y, "x": x})
    return extents, places


def shifted(value, along, by):
    extents, places = az_places(lax.axis_size("az"))
    pairs = []
    for index, place in enumerate(places):
        goal = dict(place)
        goal[along] = (place[along] + by) % extents[along]
        pairs.append((index, (goal["z"] * extents["y"] + goal["y"]) * extents["x"] + goal["x"]))
    return lax.ppermute(value, "az", pairs)


def my_place():
    extents, _ = az_places(lax.axis_size("az"))
    me = lax.axis_index("az")
    x = me % extents["x"]
    y = (me // extents["x"]) % extents["y"]
    z = me // (extents["x"] * extents["y"])
    return {"z": z, "y": y, "x": x}


def neighbour(value, az_by, grp_by):
    count = lax.axis_size("az")
    groups = lax.axis_size("grp")
    pairs = []
    for a in range(count):
        for g in range(groups):
            goal = ((a + az_by) % count) * groups + (g + grp_by) % groups
            pairs.append((a * groups + g, goal))
    return lax.ppermute(value, ("az", "grp"), pairs)


def tap_slice(ref, tap):
    return ref[:, tap * CH : (tap + 1) * CH]


def roll_rows(value, by):
    count = value.shape[0]
    rolled = pltpu.roll(value, by % count, axis=0)
    z = lax.broadcasted_iota(jnp.int32, value.shape, 0) % AXIAL
    edge = 0 if by == 1 else AXIAL - 1
    return jnp.where(z == edge, 0.0, rolled)


def shift_radius(value, by):
    layers, _, lanes = value.shape
    empty = jnp.zeros((layers, AXIAL, lanes), value.dtype)
    if by == 1:
        return jnp.concatenate([empty, value[:, : NRZ - AXIAL]], axis=1)
    return jnp.concatenate([value[:, AXIAL:], empty], axis=1)


def conv_rows(x_ref, w_ref, layers, first):
    count = layers * NRZ
    lhs = jnp.concatenate(
        [x_ref[(first + p) * NRZ : (first + p) * NRZ + count, :] for p in range(3)], axis=1
    )
    total = None
    for s in range(3):
        rhs = jnp.concatenate(
            [
                jnp.concatenate(
                    [tap_slice(w_ref, (p * 3 + q) * 3 + s) for p in range(3)], axis=1
                )
                for q in range(3)
            ],
            axis=0,
        )
        part = lax.dot_general(lhs, rhs, (((1,), (1,)), ((), ())), preferred_element_type=F32)
        part = part.reshape(layers, NRZ, 3 * LANES)
        summed = part[:, :, LANES : 2 * LANES]
        summed = summed + shift_radius(part[:, :, :LANES], 1)
        summed = summed + shift_radius(part[:, :, 2 * LANES :], -1)
        summed = summed.reshape(count, LANES)
        if s != 1:
            summed = roll_rows(summed, 1 - s)
        total = summed if total is None else total + summed
    return total


def pick_half(value, own):
    low = value[..., :LANES].astype(F32)
    high = value[..., LANES:].astype(F32)
    return jnp.where(jnp.broadcast_to(own, low.shape) == 0, low, high)


def pack_kernel(f_ref, c_ref, fc_ref, next_ref, last_ref, sems):
    copies = [
        (f_ref, fc_ref.at[:LAYERS]),
        (c_ref, fc_ref.at[LAYERS:]),
        (f_ref.at[LAYERS - 2 :], next_ref.at[:2]),
        (c_ref.at[LAYERS - 1 :], next_ref.at[2:]),
        (f_ref.at[:2], last_ref.at[:2]),
        (c_ref.at[:1], last_ref.at[2:]),
    ]
    copies = [pltpu.make_async_copy(a, b, sems.at[i]) for i, (a, b) in enumerate(copies)]
    for copy in copies:
        copy.start()
    for copy in copies:
        copy.wait()


def pack(f, c):
    return pl.pallas_call(
        pack_kernel,
        out_shape=[
            shape((2 * LAYERS, HALF, CH)),
            shape((3, HALF, CH)),
            shape((3, HALF, CH)),
        ],
        in_specs=[anywhere()] * 2,
        out_specs=[vmem()] * 3,
        scratch_shapes=[pltpu.SemaphoreType.DMA((6,))],
        compiler_params=params(),
        cost_estimate=cost(0, 900000),
    )(f, c)


def load_kernel(w1_ref, w2_ref, after, one_ref, two_ref, sems):
    copies = []
    for which, (source, goal) in enumerate(((w1_ref, one_ref), (w2_ref, two_ref))):
        for part in range(4):
            rows = pl.ds(part * 32, 32)
            copies.append(
                pltpu.make_async_copy(source.at[rows], goal.at[rows], sems.at[which, part])
            )
    for copy in copies:
        copy.start()
    for copy in copies:
        copy.wait()


def load(w_first, w_second, after):
    return pl.pallas_call(
        load_kernel,
        out_shape=[shape(w_first.shape), shape(w_second.shape)],
        in_specs=[anywhere()] * 3,
        out_specs=[vmem()] * 2,
        scratch_shapes=[pltpu.SemaphoreType.DMA((2, 4))],
        compiler_params=params(),
        cost_estimate=cost(0, 7000000),
    )(w_first, w_second, after)


def fields_kernel(
    place_ref, fc_ref, swap_ref, up_same, up_cross, down_same, down_cross,
    w1_ref, w2_ref, x_ref, cot_ref, send_ref, back_ref, slope_ref,
):
    own = place_ref[0]
    mine = pl.multiple_of(own * HALF, HALF)
    other = pl.multiple_of((1 - own) * HALF, HALF)
    for layer in range(2):
        x_ref[pl.ds(layer * NRZ + mine, HALF), :] = up_same[layer]
        x_ref[pl.ds(layer * NRZ + other, HALF), :] = up_cross[layer]
        x_ref[pl.ds((6 + layer) * NRZ + mine, HALF), :] = down_same[layer]
        x_ref[pl.ds((6 + layer) * NRZ + other, HALF), :] = down_cross[layer]
    for layer in range(LAYERS):
        x_ref[pl.ds((2 + layer) * NRZ + mine, HALF), :] = fc_ref[layer]
        x_ref[pl.ds((2 + layer) * NRZ + other, HALF), :] = swap_ref[layer]
        cot_ref[pl.ds((1 + layer) * NRZ + mine, HALF), :] = pick_half(
            fc_ref[LAYERS + layer], own
        ).astype(BF16)
        cot_ref[pl.ds((1 + layer) * NRZ + other, HALF), :] = pick_half(
            swap_ref[LAYERS + layer], own
        ).astype(BF16)
    cot_ref[pl.ds(mine, HALF), :] = pick_half(up_same[2], own).astype(BF16)
    cot_ref[pl.ds(other, HALF), :] = pick_half(up_cross[2], own).astype(BF16)
    cot_ref[pl.ds(5 * NRZ + mine, HALF), :] = pick_half(down_same[2], own).astype(BF16)
    cot_ref[pl.ds(5 * NRZ + other, HALF), :] = pick_half(down_cross[2], own).astype(BF16)

    pre = conv_rows(x_ref, w1_ref, LAYERS + 2, 0)
    sigma = jax.nn.sigmoid(pre)
    send_ref[: (LAYERS + 2) * NRZ, :] = (pre * sigma).astype(BF16)
    inner = pre[NRZ : NRZ * (LAYERS + 1)]
    sigma = sigma[NRZ : NRZ * (LAYERS + 1)]
    slope_ref[...] = sigma * (1.0 + inner * (1.0 - sigma))

    count = LAYERS * NRZ
    lhs = jnp.concatenate(
        [cot_ref[(2 - p) * NRZ : (2 - p) * NRZ + count, :] for p in range(3)], axis=1
    )
    total = None
    for s in range(3):
        summed = None
        for q in range(3):
            rhs = jnp.concatenate(
                [tap_slice(w2_ref, (p * 3 + q) * 3 + s) for p in range(3)], axis=0
            )
            part = jnp.dot(lhs, rhs, preferred_element_type=F32).reshape(LAYERS, NRZ, CH)
            if q != 1:
                part = shift_radius(part, q - 1)
            summed = part if summed is None else summed + part
        summed = summed.reshape(count, CH)
        if s != 1:
            summed = roll_rows(summed, s - 1)
        total = summed if total is None else total + summed
    back_ref[...] = pick_half(total, own)
    send_ref[(LAYERS + 2) * NRZ :, :] = pick_half(total, 1 - own).astype(BF16)


def fields(place, fc, swap, halos, w_first, w_second):
    rows = (LAYERS + 2) * NRZ
    return pl.pallas_call(
        fields_kernel,
        out_shape=[
            shape(((LAYERS + 4) * NRZ, CH)),
            shape((rows, LANES)),
            shape((rows + LAYERS * NRZ, LANES)),
            shape((LAYERS * NRZ, LANES), F32),
            shape((LAYERS * NRZ, LANES), F32),
        ],
        in_specs=[smem()] + [vmem()] * 8,
        out_specs=[vmem()] * 5,
        compiler_params=params(),
        cost_estimate=cost(2300000000, 6000000),
    )(place, fc, swap, *halos, w_first, w_second)


def grad_pieces(place_ref, source, field, factor, turned_ref, outs):
    own_x = place_ref[1]
    own_y = place_ref[2]
    own_z = place_ref[3]
    keep, y_first, y_last, x_first, x_last, d_first, d_last = outs
    lane = lax.broadcasted_iota(jnp.int32, (LANES, NRZ), 1)
    z = lane % AXIAL
    r = lane // AXIAL
    for layer in range(LAYERS):
        turned = source[layer * NRZ : (layer + 1) * NRZ, :].T
        for q in range(3):
            for s in range(3):
                by = AXIAL * (q - 1) + (s - 1)
                moved = pltpu.roll(turned, by % NRZ, axis=1) if by else turned
                if q == 0:
                    moved = jnp.where(r == NRZ // AXIAL - 1, 0.0, moved)
                if q == 2:
                    moved = jnp.where(r == 0, 0.0, moved)
                if s == 0:
                    moved = jnp.where(z == AXIAL - 1, 0.0, moved)
                if s == 2:
                    moved = jnp.where(z == 0, 0.0, moved)
                row = (q * 3 + s) * LANES
                turned_ref[row : row + LANES, layer * NRZ : (layer + 1) * NRZ] = moved.astype(BF16)
    x_zero = jnp.broadcast_to(own_x, (LANES, LANES)) == 0
    y_zero = jnp.broadcast_to(own_y, (HALF, LANES)) == 0
    slots = [lax.rem(index - own_z + 4, 4) for index in range(4)]
    for p in range(3):
        product = jnp.dot(turned_ref[...], field(p), preferred_element_type=F32) * factor
        for within in range(9):
            tap = p * 9 + within
            value = product[within * LANES : (within + 1) * LANES]
            low = value[:, :LANES]
            high = value[:, LANES:]
            halves = (jnp.where(x_zero, low, high), jnp.where(x_zero, high, low))
            for dx in range(2):
                top = halves[dx][:HALF]
                bottom = halves[dx][HALF:]
                parts = (jnp.where(y_zero, top, bottom), jnp.where(y_zero, bottom, top))
                for dy in range(2):
                    if dx == 0 and dy == 0:
                        ref, row = keep, tap * BLOCK
                    else:
                        pair = {(1, 0): (x_first, x_last), (0, 1): (y_first, y_last)}.get(
                            (dx, dy), (d_first, d_last)
                        )
                        if tap < FIRST_TAPS:
                            ref, row = pair[0], tap * BLOCK
                        else:
                            ref, row = pair[1], (tap - FIRST_TAPS) * BLOCK
                    narrow = parts[dy].astype(BF16)
                    for index in range(4):
                        ref[slots[index], row : row + BLOCK, :] = narrow[
                            index * BLOCK : (index + 1) * BLOCK
                        ]


def second_kernel(factor, place_ref, cot_ref, send_ref, got_ref, h_ref, *rest):
    outs, turned_ref = rest[:7], rest[7]
    rows = (LAYERS + 2) * NRZ
    own = place_ref[0]
    mine = send_ref[:rows, :].astype(F32)
    other = got_ref[:rows, :].astype(F32)
    first = jnp.broadcast_to(own, mine.shape) == 0
    h_ref[:, :LANES] = jnp.where(first, mine, other).astype(BF16)
    h_ref[:, LANES:] = jnp.where(first, other, mine).astype(BF16)
    source = cot_ref[NRZ : NRZ * (LAYERS + 1), :].astype(F32)
    field = lambda p: h_ref[p * NRZ : p * NRZ + LAYERS * NRZ, :]
    grad_pieces(place_ref, source, field, factor, turned_ref, outs)


def first_kernel(factor, place_ref, back_ref, got_ref, slope_ref, x_ref, after, *rest):
    outs, turned_ref = rest[:7], rest[7]
    rows = (LAYERS + 2) * NRZ
    source = (back_ref[...] + got_ref[rows:, :].astype(F32)) * slope_ref[...]
    source = source.astype(BF16).astype(F32)
    field = lambda p: x_ref[(p + 1) * NRZ : (p + 1) * NRZ + LAYERS * NRZ, :]
    grad_pieces(place_ref, source, field, factor, turned_ref, outs)


def piece_shapes():
    return [shape((4, ROWS, LANES))] + [shape((4, FIRST, LANES)), shape((4, LAST, LANES))] * 3


def second_grad(place, factor, cot, send, got):
    outs = pl.pallas_call(
        functools.partial(second_kernel, factor),
        out_shape=[shape(((LAYERS + 2) * NRZ, CH))] + piece_shapes(),
        in_specs=[smem()] + [vmem()] * 3,
        out_specs=[vmem()] * 8,
        scratch_shapes=[pltpu.VMEM((9 * LANES, LAYERS * NRZ), BF16)],
        compiler_params=params(),
        cost_estimate=cost(1000000000, 3000000),
    )(place, cot, send, got)
    return outs[0], outs[1:]


def first_grad(place, factor, back, got, slope, x, after):
    return pl.pallas_call(
        functools.partial(first_kernel, factor),
        out_shape=piece_shapes(),
        in_specs=[smem()] + [vmem()] * 4 + [anywhere()],
        out_specs=[vmem()] * 7,
        scratch_shapes=[pltpu.VMEM((9 * LANES, LAYERS * NRZ), BF16)],
        compiler_params=params(),
        cost_estimate=cost(1000000000, 3000000),
    )(place, back, got, slope, x, after)


def flow_kernel(place_ref, x_ref, h_ref, w2_ref, keep_ref, send_ref):
    own = place_ref[0]
    result = conv_rows(h_ref, w2_ref, LAYERS, 0)
    result = result + pick_half(x_ref[2 * NRZ : 2 * NRZ + LAYERS * NRZ, :], own)
    halves = result.reshape(LAYERS, 2, HALF, LANES)
    first = jnp.broadcast_to(own, (LAYERS, HALF, LANES)) == 0
    keep_ref[...] = jnp.where(first, halves[:, 0], halves[:, 1]).astype(BF16)
    send_ref[...] = jnp.where(first, halves[:, 1], halves[:, 0]).astype(BF16)


def flow(place, x, h, w_second):
    return pl.pallas_call(
        flow_kernel,
        out_shape=[shape((LAYERS, HALF, LANES))] * 2,
        in_specs=[smem()] + [vmem()] * 3,
        out_specs=[vmem()] * 2,
        compiler_params=params(),
        cost_estimate=cost(1000000000, 3000000),
    )(place, x, h, w_second)


def join_kernel(place_ref, mine_ref, theirs_ref, out_ref):
    mine = mine_ref[...].astype(F32)
    theirs = theirs_ref[...].astype(F32)
    first = jnp.broadcast_to(place_ref[0], mine.shape) == 0
    out_ref[:, :, :LANES] = jnp.where(first, mine, theirs).astype(BF16)
    out_ref[:, :, LANES:] = jnp.where(first, theirs, mine).astype(BF16)


def join_flow(place, mine, theirs):
    return pl.pallas_call(
        join_kernel,
        out_shape=shape((LAYERS, HALF, CH)),
        in_specs=[smem()] + [vmem()] * 2,
        out_specs=vmem(),
        compiler_params=params(),
        cost_estimate=cost(0, 400000),
    )(place, mine, theirs)


def write_kernel(place_ref, m_ref, mx_ref, my_ref, first_ref, last_ref, out_ref):
    x_zero = jnp.broadcast_to(place_ref[1], (BLOCK, LANES)) == 0
    far = pl.program_id(0)

    def put(tap, near, across):
        low = jnp.where(x_zero, near, across)
        high = jnp.where(x_zero, across, near)
        out_ref[:, tap * CH : tap * CH + LANES] = low
        out_ref[:, tap * CH + LANES : (tap + 1) * CH] = high

    @pl.when(far == 0)
    def _():
        for tap in range(TAPS):
            rows = slice(tap * BLOCK, (tap + 1) * BLOCK)
            put(tap, m_ref[0, rows, :].astype(F32), mx_ref[0, rows, :].astype(F32))

    @pl.when(far == 1)
    def _():
        for tap in range(TAPS):
            rows = slice(tap * BLOCK, (tap + 1) * BLOCK)
            if tap < FIRST_TAPS:
                across = first_ref[0, rows, :]
            else:
                across = last_ref[0, (tap - FIRST_TAPS) * BLOCK : (tap - FIRST_TAPS + 1) * BLOCK, :]
            put(tap, my_ref[0, rows, :].astype(F32), across.astype(F32))


def write_out(place, pieces):
    near = lambda dy, dz, place: (dz * (1 - dy) + 3 * dy, 0, 0)
    far = lambda dy, dz, place: (dz * dy, 0, 0)
    block = lambda dy, dz, place: (
        lax.rem(place[2] + dy, 2) * 4 + lax.rem(place[3] + dz, 4),
        0,
    )
    return pl.pallas_call(
        write_kernel,
        out_shape=shape((LANES, TAPS * CH), F32),
        grid_spec=pltpu.PrefetchScalarGridSpec(
            num_scalar_prefetch=1,
            grid=(2, 4),
            in_specs=[
                pl.BlockSpec((1, ROWS, LANES), near),
                pl.BlockSpec((1, ROWS, LANES), near),
                pl.BlockSpec((1, ROWS, LANES), far),
                pl.BlockSpec((1, FIRST, LANES), far),
                pl.BlockSpec((1, LAST, LANES), far),
            ],
            out_specs=pl.BlockSpec((BLOCK, TAPS * CH), block),
        ),
        compiler_params=params(),
        cost_estimate=cost(0, 6000000),
    )(place, *pieces)


def plus(*terms):
    total = terms[0].astype(F32)
    for term in terms[1:]:
        total = total + term.astype(F32)
    return total.astype(BF16)


def meet_kernel(y_first, got_first, x_last, got_last, after, y_out, x_out):
    y_out[...] = plus(y_first[...], got_first[...])
    x_out[...] = plus(x_last[...], got_last[...])


def meet(y_first, got_first, x_last, got_last, after):
    return pl.pallas_call(
        meet_kernel,
        out_shape=[shape(y_first.shape), shape(x_last.shape)],
        in_specs=[vmem()] * 4 + [anywhere()],
        out_specs=[vmem()] * 2,
        compiler_params=params(),
        cost_estimate=cost(0, 1300000),
    )(y_first, got_first, x_last, got_last, after)


def sum_kernel(keep, x_first, x_last, y_first, y_last, after, *outs):
    for index in range(4):
        for rows, x_part, y_part in (
            (slice(0, FIRST), x_first, y_first),
            (slice(FIRST, ROWS), x_last, y_last),
        ):
            outs[index][rows, :] = plus(keep[index, rows, :], x_part[index], y_part[index])


def sum_quads(keep, x_first, x_last, y_first, y_last, after):
    return pl.pallas_call(
        sum_kernel,
        out_shape=[shape((ROWS, LANES))] * 4,
        in_specs=[vmem()] * 5 + [anywhere()],
        out_specs=[vmem()] * 4,
        compiler_params=params(),
        cost_estimate=cost(0, 1800000),
    )(keep, x_first, x_last, y_first, y_last, after)


def own_kernel(one, two, three, four, after, out):
    out[...] = plus(one[...], two[...], three[...], four[...])


def own_block(rows, after):
    return pl.pallas_call(
        own_kernel,
        out_shape=shape((ROWS, LANES)),
        in_specs=[vmem()] * 4 + [anywhere()],
        out_specs=vmem(),
        compiler_params=params(),
        cost_estimate=cost(0, 600000),
    )(*rows, after)


def stack_kernel(one, two, three, four, after, out):
    for index, ref in enumerate((one, two, three, four)):
        out[index] = ref[...]


def stack_blocks(rows, after):
    return pl.pallas_call(
        stack_kernel,
        out_shape=shape((4, ROWS, LANES)),
        in_specs=[vmem()] * 4 + [anywhere()],
        out_specs=vmem(),
        compiler_params=params(),
        cost_estimate=cost(0, 900000),
    )(*rows, after)


def relay_kernel(x_ref, y_ref, after, first_ref, last_ref):
    first_ref[...] = x_ref[:, :FIRST]
    last_ref[...] = y_ref[:, FIRST:]


def relay(across_x, across_y, after):
    return pl.pallas_call(
        relay_kernel,
        out_shape=[shape((4, FIRST, LANES)), shape((4, LAST, LANES))],
        in_specs=[vmem()] * 2 + [anywhere()],
        out_specs=[vmem()] * 2,
        compiler_params=params(),
        cost_estimate=cost(0, 900000),
    )(across_x, across_y, after)


class QuadSum:
    def diagonal(self, pieces):
        self.keep, self.y_first, self.y_last, self.x_first, self.x_last, d_first, d_last = pieces
        self.got_first = shifted(d_first, "x", 1)
        self.got_last = shifted(d_last, "y", 1)
        self.in_x_first = shifted(self.x_first, "x", 1)
        self.in_y_last = shifted(self.y_last, "y", 1)

    def sides(self, after):
        y_first, x_last = meet(self.y_first, self.got_first, self.x_last, self.got_last, after)
        self.in_y_first = shifted(y_first, "y", 1)
        self.in_x_last = shifted(x_last, "x", 1)
        return x_last

    def along_z(self, after):
        rows = sum_quads(
            self.keep, self.in_x_first, self.in_x_last, self.in_y_first, self.in_y_last, after
        )
        self.rows = [rows[0]] + [shifted(rows[by], "z", by) for by in range(1, 4)]
        return rows[0]

    def back_z(self, after):
        own = own_block(self.rows, after)
        self.blocks = [own] + [shifted(own, "z", -by) for by in range(1, 4)]
        return own

    def back_sides(self, after):
        self.whole = stack_blocks(self.blocks, after)
        self.across_x = shifted(self.whole, "x", 1)
        self.across_y = shifted(self.whole, "y", 1)
        return self.whole

    def back_diagonal(self, after):
        first, last = relay(self.across_x, self.across_y, after)
        self.far_first = shifted(first, "y", 1)
        self.far_last = shifted(last, "x", 1)
        return last

    def result(self):
        return self.whole, self.across_x, self.across_y, self.far_first, self.far_last


def any_reduce_gather(pieces, place):
    extents, _ = az_places(lax.axis_size("az"))
    count = lax.axis_size("az")
    keep, y_first, y_last, x_first, x_last, d_first, d_last = pieces
    join = lambda first, last: jnp.concatenate([first, last], axis=1)
    cut = jnp.stack([keep, join(y_first, y_last), join(x_first, x_last), join(d_first, d_last)])
    order = ("x", "y", "z")
    full = cut.shape
    cut = cut.reshape([extents[name] for name in order] + [-1, LANES])
    for position, name in enumerate(order):
        cut = jnp.roll(cut, -place[name], axis=position)
    for name in order:
        cut = plus(cut[0], *[shifted(cut[by], name, by) for by in range(1, extents[name])])
    for name in order[::-1]:
        mine = cut
        cut = jnp.stack([mine] + [shifted(mine, name, -by) for by in range(1, extents[name])])
    for position, name in enumerate(order):
        cut = jnp.roll(cut, place[name], axis=position)
    cut = cut.reshape(full)
    return cut[0], cut[2], cut[1], cut[3][:, :FIRST], cut[3][:, FIRST:]


def local(features, cotangent, w_first, w_second):
    groups = lax.axis_size("grp")
    cells = lax.axis_size("az") * LAYERS * HALF * groups
    factor = 1.0 / math.sqrt(cells)
    extents, _ = az_places(lax.axis_size("az"))
    quad = extents == {"x": 2, "y": 2, "z": 4}
    spot = my_place()
    own = lax.axis_index("grp")
    zero = jnp.zeros((), jnp.int32)
    place = jnp.stack(
        [own] + [spot[name] if quad else zero for name in ("x", "y", "z")]
    ).astype(jnp.int32)

    f = features.transpose(1, 2, 0)
    c = cotangent.transpose(1, 2, 0)
    fc, to_next, to_last = pack(f, c)
    swap = neighbour(fc, 0, 1)
    up = neighbour(to_next, 1, 0)
    down = neighbour(to_last, -1, 0)
    w_one, w_two = load(w_first, w_second, to_last)
    halos = [up, neighbour(up, 0, 1), down, neighbour(down, 0, 1)]
    x, cot, send, back, slope = fields(place, fc, swap, halos, w_one, w_two)
    got = neighbour(send, 0, 1)
    hidden, second = second_grad(place, factor, cot, send, got)
    mine, theirs = flow(place, x, hidden, w_two)
    theirs = neighbour(theirs, 0, 1)
    if quad:
        one, two = QuadSum(), QuadSum()
        one.diagonal(second)
        step = one.sides(mine)
        two.diagonal(first_grad(place, factor, back, got, slope, x, step))
        flow_out = join_flow(place, mine, theirs)
        step = one.along_z(flow_out)
        step = two.sides(step)
        step = one.back_z(step)
        step = two.along_z(step)
        step = one.back_sides(step)
        step = two.back_z(step)
        step = one.back_diagonal(step)
        step = two.back_sides(step)
        grad_second = write_out(place, one.result())
        two.back_diagonal(grad_second)
        grad_first = write_out(place, two.result())
    else:
        flow_out = join_flow(place, mine, theirs)
        first = first_grad(place, factor, back, got, slope, x, mine)
        grad_second = write_out(place, any_reduce_gather(second, spot))
        grad_first = write_out(place, any_reduce_gather(first, spot))
    return (flow_out.transpose(2, 0, 1), grad_first, grad_second)


def solution(mesh):
    in_specs = (P(None, "az", "grp"), P(None, "az", "grp"), P("grp", None), P("grp", None))
    out_specs = (P(None, "az", "grp"), P("grp", None), P("grp", None))
    return jax.shard_map(local, mesh=mesh, in_specs=in_specs, out_specs=out_specs, check_vma=False)
```

```python
import functools
import math

import jax
import jax.numpy as jnp
from jax import lax
from jax.experimental import pallas as pl
from jax.experimental.pallas import tpu as pltpu
from jax.sharding import PartitionSpec as P

AXIAL = 8
NRZ = 128
HALF = 64
LANES = 128
CH = 256
LAYERS = 4
TAPS = 27
BLOCK = 16
FIRST_TAPS = 14
ROWS = TAPS * BLOCK
FIRST = FIRST_TAPS * BLOCK
LAST = ROWS - FIRST
VMEM_LIMIT = 40 * 1024 * 1024
BF16 = jnp.bfloat16
F32 = jnp.float32


def params():
    return pltpu.CompilerParams(vmem_limit_bytes=VMEM_LIMIT)


def vmem():
    return pl.BlockSpec(memory_space=pltpu.VMEM)


def anywhere():
    return pl.BlockSpec(memory_space=pl.ANY)


def in_hbm():
    return pl.BlockSpec(memory_space=pltpu.HBM)


def smem():
    return pl.BlockSpec(memory_space=pltpu.SMEM)


def shape(dims, kind=BF16):
    return jax.ShapeDtypeStruct(dims, kind)


def cost(flops, moved):
    return pl.CostEstimate(flops=flops, bytes_accessed=moved, transcendentals=0)


def az_extents(count):
    side = 1
    while (2 * side) ** 3 <= count:
        side *= 2
    if count % (side * side):
        side = 1
    return {"z": count // (side * side), "y": side, "x": side}


def az_places(count):
    extents = az_extents(count)
    places = []
    for index in range(count):
        rest, x = divmod(index, extents["x"])
        z, y = divmod(rest, extents["y"])
        places.append({"z": z, "y": y, "x": x})
    return extents, places


def shifted(value, along, by):
    extents, places = az_places(lax.axis_size("az"))
    pairs = []
    for index, place in enumerate(places):
        goal = dict(place)
        goal[along] = (place[along] + by) % extents[along]
        pairs.append((index, (goal["z"] * extents["y"] + goal["y"]) * extents["x"] + goal["x"]))
    return lax.ppermute(value, "az", pairs)


def my_place():
    extents, _ = az_places(lax.axis_size("az"))
    me = lax.axis_index("az")
    x = me % extents["x"]
    y = (me // extents["x"]) % extents["y"]
    z = me // (extents["x"] * extents["y"])
    return {"z": z, "y": y, "x": x}


def neighbour(value, az_by, grp_by):
    count = lax.axis_size("az")
    groups = lax.axis_size("grp")
    pairs = []
    for a in range(count):
        for g in range(groups):
            goal = ((a + az_by) % count) * groups + (g + grp_by) % groups
            pairs.append((a * groups + g, goal))
    return lax.ppermute(value, ("az", "grp"), pairs)


def tap_slice(ref, tap):
    return ref[:, tap * CH : (tap + 1) * CH]


def roll_rows(value, by):
    count = value.shape[0]
    rolled = pltpu.roll(value, by % count, axis=0)
    z = lax.broadcasted_iota(jnp.int32, value.shape, 0) % AXIAL
    edge = 0 if by == 1 else AXIAL - 1
    return jnp.where(z == edge, 0.0, rolled)


def shift_radius(value, by):
    layers, _, lanes = value.shape
    empty = jnp.zeros((layers, AXIAL, lanes), value.dtype)
    if by == 1:
        return jnp.concatenate([empty, value[:, : NRZ - AXIAL]], axis=1)
    return jnp.concatenate([value[:, AXIAL:], empty], axis=1)


def conv_rows(x_ref, w_ref, layers, first):
    count = layers * NRZ
    lhs = jnp.concatenate(
        [x_ref[(first + p) * NRZ : (first + p) * NRZ + count, :] for p in range(3)], axis=1
    )
    total = None
    for s in range(3):
        rhs = jnp.concatenate(
            [
                jnp.concatenate(
                    [tap_slice(w_ref, (p * 3 + q) * 3 + s) for p in range(3)], axis=1
                )
                for q in range(3)
            ],
            axis=0,
        )
        part = lax.dot_general(lhs, rhs, (((1,), (1,)), ((), ())), preferred_element_type=F32)
        part = part.reshape(layers, NRZ, 3 * LANES)
        summed = part[:, :, LANES : 2 * LANES]
        summed = summed + shift_radius(part[:, :, :LANES], 1)
        summed = summed + shift_radius(part[:, :, 2 * LANES :], -1)
        summed = summed.reshape(count, LANES)
        if s != 1:
            summed = roll_rows(summed, 1 - s)
        total = summed if total is None else total + summed
    return total


def pick_half(value, own):
    low = value[..., :LANES].astype(F32)
    high = value[..., LANES:].astype(F32)
    return jnp.where(jnp.broadcast_to(own, low.shape) == 0, low, high)


def pack_kernel(f_ref, c_ref, fc_ref, next_ref, last_ref, sems):
    copies = [
        (f_ref, fc_ref.at[:LAYERS]),
        (c_ref, fc_ref.at[LAYERS:]),
        (f_ref.at[LAYERS - 2 :], next_ref.at[:2]),
        (c_ref.at[LAYERS - 1 :], next_ref.at[2:]),
        (f_ref.at[:2], last_ref.at[:2]),
        (c_ref.at[:1], last_ref.at[2:]),
    ]
    copies = [pltpu.make_async_copy(a, b, sems.at[i]) for i, (a, b) in enumerate(copies)]
    for copy in copies:
        copy.start()
    for copy in copies:
        copy.wait()


def pack(f, c):
    return pl.pallas_call(
        pack_kernel,
        out_shape=[
            shape((2 * LAYERS, HALF, CH)),
            shape((3, HALF, CH)),
            shape((3, HALF, CH)),
        ],
        in_specs=[in_hbm()] * 2,
        out_specs=[vmem()] * 3,
        scratch_shapes=[pltpu.SemaphoreType.DMA((6,))],
        compiler_params=params(),
        cost_estimate=cost(0, 900000),
    )(f, c)


def load_kernel(w1_ref, w2_ref, after, one_ref, two_ref, sems):
    copies = []
    for which, (source, goal) in enumerate(((w1_ref, one_ref), (w2_ref, two_ref))):
        for part in range(4):
            rows = pl.ds(part * 32, 32)
            copies.append(
                pltpu.make_async_copy(source.at[rows], goal.at[rows], sems.at[which, part])
            )
    for copy in copies:
        copy.start()
    for copy in copies:
        copy.wait()


def load(w_first, w_second, after):
    return pl.pallas_call(
        load_kernel,
        out_shape=[shape(w_first.shape), shape(w_second.shape)],
        in_specs=[in_hbm()] * 2 + [anywhere()],
        out_specs=[vmem()] * 2,
        scratch_shapes=[pltpu.SemaphoreType.DMA((2, 4))],
        compiler_params=params(),
        cost_estimate=cost(0, 7000000),
    )(w_first, w_second, after)


def fields_kernel(
    place_ref, fc_ref, swap_ref, up_same, up_cross, down_same, down_cross,
    w1_ref, w2_ref, x_ref, cot_ref, send_ref, back_ref, slope_ref,
):
    own = place_ref[0]
    mine = pl.multiple_of(own * HALF, HALF)
    other = pl.multiple_of((1 - own) * HALF, HALF)
    for layer in range(2):
        x_ref[pl.ds(layer * NRZ + mine, HALF), :] = up_same[layer]
        x_ref[pl.ds(layer * NRZ + other, HALF), :] = up_cross[layer]
        x_ref[pl.ds((6 + layer) * NRZ + mine, HALF), :] = down_same[layer]
        x_ref[pl.ds((6 + layer) * NRZ + other, HALF), :] = down_cross[layer]
    for layer in range(LAYERS):
        x_ref[pl.ds((2 + layer) * NRZ + mine, HALF), :] = fc_ref[layer]
        x_ref[pl.ds((2 + layer) * NRZ + other, HALF), :] = swap_ref[layer]
        cot_ref[pl.ds((1 + layer) * NRZ + mine, HALF), :] = pick_half(
            fc_ref[LAYERS + layer], own
        ).astype(BF16)
        cot_ref[pl.ds((1 + layer) * NRZ + other, HALF), :] = pick_half(
            swap_ref[LAYERS + layer], own
        ).astype(BF16)
    cot_ref[pl.ds(mine, HALF), :] = pick_half(up_same[2], own).astype(BF16)
    cot_ref[pl.ds(other, HALF), :] = pick_half(up_cross[2], own).astype(BF16)
    cot_ref[pl.ds(5 * NRZ + mine, HALF), :] = pick_half(down_same[2], own).astype(BF16)
    cot_ref[pl.ds(5 * NRZ + other, HALF), :] = pick_half(down_cross[2], own).astype(BF16)

    pre = conv_rows(x_ref, w1_ref, LAYERS + 2, 0)
    sigma = jax.nn.sigmoid(pre)
    send_ref[: (LAYERS + 2) * NRZ, :] = (pre * sigma).astype(BF16)
    inner = pre[NRZ : NRZ * (LAYERS + 1)]
    sigma = sigma[NRZ : NRZ * (LAYERS + 1)]
    slope_ref[...] = sigma * (1.0 + inner * (1.0 - sigma))

    count = LAYERS * NRZ
    lhs = jnp.concatenate(
        [cot_ref[(2 - p) * NRZ : (2 - p) * NRZ + count, :] for p in range(3)], axis=1
    )
    total = None
    for s in range(3):
        summed = None
        for q in range(3):
            rhs = jnp.concatenate(
                [tap_slice(w2_ref, (p * 3 + q) * 3 + s) for p in range(3)], axis=0
            )
            part = jnp.dot(lhs, rhs, preferred_element_type=F32).reshape(LAYERS, NRZ, CH)
            if q != 1:
                part = shift_radius(part, q - 1)
            summed = part if summed is None else summed + part
        summed = summed.reshape(count, CH)
        if s != 1:
            summed = roll_rows(summed, s - 1)
        total = summed if total is None else total + summed
    back_ref[...] = pick_half(total, own)
    send_ref[(LAYERS + 2) * NRZ :, :] = pick_half(total, 1 - own).astype(BF16)


def fields(place, fc, swap, halos, w_first, w_second):
    rows = (LAYERS + 2) * NRZ
    return pl.pallas_call(
        fields_kernel,
        out_shape=[
            shape(((LAYERS + 4) * NRZ, CH)),
            shape((rows, LANES)),
            shape((rows + LAYERS * NRZ, LANES)),
            shape((LAYERS * NRZ, LANES), F32),
            shape((LAYERS * NRZ, LANES), F32),
        ],
        in_specs=[smem()] + [vmem()] * 8,
        out_specs=[vmem()] * 5,
        compiler_params=params(),
        cost_estimate=cost(2300000000, 6000000),
    )(place, fc, swap, *halos, w_first, w_second)


def grad_pieces(place_ref, source, field, factor, turned_ref, outs):
    own_x = place_ref[1]
    own_y = place_ref[2]
    own_z = place_ref[3]
    keep, y_first, x_last, x_both, y_both = outs
    lane = lax.broadcasted_iota(jnp.int32, (LANES, NRZ), 1)
    z = lane % AXIAL
    r = lane // AXIAL
    for layer in range(LAYERS):
        turned = source[layer * NRZ : (layer + 1) * NRZ, :].T
        for q in range(3):
            for s in range(3):
                by = AXIAL * (q - 1) + (s - 1)
                moved = pltpu.roll(turned, by % NRZ, axis=1) if by else turned
                if q == 0:
                    moved = jnp.where(r == NRZ // AXIAL - 1, 0.0, moved)
                if q == 2:
                    moved = jnp.where(r == 0, 0.0, moved)
                if s == 0:
                    moved = jnp.where(z == AXIAL - 1, 0.0, moved)
                if s == 2:
                    moved = jnp.where(z == 0, 0.0, moved)
                row = (q * 3 + s) * LANES
                turned_ref[row : row + LANES, layer * NRZ : (layer + 1) * NRZ] = moved.astype(BF16)
    x_zero = jnp.broadcast_to(own_x, (LANES, LANES)) == 0
    y_zero = jnp.broadcast_to(own_y, (HALF, LANES)) == 0
    slots = [lax.rem(index - own_z + 4, 4) for index in range(4)]
    for p in range(3):
        product = jnp.dot(turned_ref[...], field(p), preferred_element_type=F32) * factor
        for within in range(9):
            tap = p * 9 + within
            value = product[within * LANES : (within + 1) * LANES]
            low = value[:, :LANES]
            high = value[:, LANES:]
            halves = (jnp.where(x_zero, low, high), jnp.where(x_zero, high, low))
            for dx in range(2):
                top = halves[dx][:HALF]
                bottom = halves[dx][HALF:]
                parts = (jnp.where(y_zero, top, bottom), jnp.where(y_zero, bottom, top))
                for dy in range(2):
                    early = tap < FIRST_TAPS
                    row = (tap if early else tap - FIRST_TAPS) * BLOCK
                    if dx == 0 and dy == 0:
                        ref, row = keep, tap * BLOCK
                    elif dx == 1 and dy == 1:
                        ref = x_both if early else y_both
                    elif dx == 1:
                        ref, row = (x_both, FIRST + row) if early else (x_last, row)
                    else:
                        ref, row = (y_first, row) if early else (y_both, LAST + row)
                    narrow = parts[dy].astype(BF16)
                    for index in range(4):
                        ref[slots[index], row : row + BLOCK, :] = narrow[
                            index * BLOCK : (index + 1) * BLOCK
                        ]


def second_kernel(factor, place_ref, cot_ref, send_ref, got_ref, h_ref, *rest):
    outs, turned_ref = rest[:5], rest[5]
    rows = (LAYERS + 2) * NRZ
    own = place_ref[0]
    mine = send_ref[:rows, :].astype(F32)
    other = got_ref[:rows, :].astype(F32)
    first = jnp.broadcast_to(own, mine.shape) == 0
    h_ref[:, :LANES] = jnp.where(first, mine, other).astype(BF16)
    h_ref[:, LANES:] = jnp.where(first, other, mine).astype(BF16)
    source = cot_ref[NRZ : NRZ * (LAYERS + 1), :].astype(F32)
    field = lambda p: h_ref[p * NRZ : p * NRZ + LAYERS * NRZ, :]
    grad_pieces(place_ref, source, field, factor, turned_ref, outs)


def first_kernel(factor, place_ref, back_ref, got_ref, slope_ref, x_ref, after, *rest):
    outs, turned_ref = rest[:5], rest[5]
    rows = (LAYERS + 2) * NRZ
    source = (back_ref[...] + got_ref[rows:, :].astype(F32)) * slope_ref[...]
    source = source.astype(BF16).astype(F32)
    field = lambda p: x_ref[(p + 1) * NRZ : (p + 1) * NRZ + LAYERS * NRZ, :]
    grad_pieces(place_ref, source, field, factor, turned_ref, outs)


def piece_shapes():
    return [shape((4, rows, LANES)) for rows in (ROWS, FIRST, LAST, 2 * FIRST, 2 * LAST)]


def second_grad(place, factor, cot, send, got):
    outs = pl.pallas_call(
        functools.partial(second_kernel, factor),
        out_shape=[shape(((LAYERS + 2) * NRZ, CH))] + piece_shapes(),
        in_specs=[smem()] + [vmem()] * 3,
        out_specs=[vmem()] * 6,
        scratch_shapes=[pltpu.VMEM((9 * LANES, LAYERS * NRZ), BF16)],
        compiler_params=params(),
        cost_estimate=cost(1000000000, 3000000),
    )(place, cot, send, got)
    return outs[0], outs[1:]


def first_grad(place, factor, back, got, slope, x, after):
    return pl.pallas_call(
        functools.partial(first_kernel, factor),
        out_shape=piece_shapes(),
        in_specs=[smem()] + [vmem()] * 4 + [anywhere()],
        out_specs=[vmem()] * 5,
        scratch_shapes=[pltpu.VMEM((9 * LANES, LAYERS * NRZ), BF16)],
        compiler_params=params(),
        cost_estimate=cost(1000000000, 3000000),
    )(place, back, got, slope, x, after)


def flow_kernel(place_ref, x_ref, h_ref, w2_ref, keep_ref, send_ref):
    own = place_ref[0]
    result = conv_rows(h_ref, w2_ref, LAYERS, 0)
    result = result + pick_half(x_ref[2 * NRZ : 2 * NRZ + LAYERS * NRZ, :], own)
    halves = result.reshape(LAYERS, 2, HALF, LANES)
    first = jnp.broadcast_to(own, (LAYERS, HALF, LANES)) == 0
    keep_ref[...] = jnp.where(first, halves[:, 0], halves[:, 1]).astype(BF16)
    send_ref[...] = jnp.where(first, halves[:, 1], halves[:, 0]).astype(BF16)


def flow(place, x, h, w_second):
    return pl.pallas_call(
        flow_kernel,
        out_shape=[shape((LAYERS, HALF, LANES))] * 2,
        in_specs=[smem()] + [vmem()] * 3,
        out_specs=[vmem()] * 2,
        compiler_params=params(),
        cost_estimate=cost(1000000000, 3000000),
    )(place, x, h, w_second)


def join_kernel(place_ref, mine_ref, theirs_ref, out_ref, token_ref):
    token_ref[...] = jnp.zeros_like(token_ref)
    mine = mine_ref[...].astype(F32)
    theirs = theirs_ref[...].astype(F32)
    first = jnp.broadcast_to(place_ref[0], mine.shape) == 0
    out_ref[:, :, :LANES] = jnp.where(first, mine, theirs).astype(BF16)
    out_ref[:, :, LANES:] = jnp.where(first, theirs, mine).astype(BF16)


def join_flow(place, mine, theirs):
    return pl.pallas_call(
        join_kernel,
        out_shape=[shape((LAYERS, HALF, CH)), shape((8, LANES), F32)],
        in_specs=[smem()] + [vmem()] * 2,
        out_specs=[vmem()] * 2,
        compiler_params=params(),
        cost_estimate=cost(0, 400000),
    )(place, mine, theirs)


def write_kernel(
    place_ref, m_ref, mx_ref, my_ref, first_ref, last_ref, after, out_ref, token_ref, block_ref, sems
):
    token_ref[...] = jnp.zeros_like(token_ref)
    x_zero = jnp.broadcast_to(place_ref[1], (BLOCK, LANES)) == 0
    copies = []
    for dy in range(2):
        for dz in range(4):
            index = dy * 4 + dz
            for tap in range(TAPS):
                rows = slice(tap * BLOCK, (tap + 1) * BLOCK)
                if dy == 0:
                    near, across = m_ref[dz, rows, :], mx_ref[dz, rows, :]
                elif tap < FIRST_TAPS:
                    near, across = my_ref[dz, rows, :], first_ref[dz, rows, :]
                else:
                    late = slice((tap - FIRST_TAPS) * BLOCK, (tap - FIRST_TAPS + 1) * BLOCK)
                    near, across = my_ref[dz, rows, :], last_ref[dz, late, :]
                near = near.astype(F32)
                across = across.astype(F32)
                block_ref[index, :, tap * CH : tap * CH + LANES] = jnp.where(x_zero, near, across)
                block_ref[index, :, tap * CH + LANES : (tap + 1) * CH] = jnp.where(
                    x_zero, across, near
                )
            row = lax.rem(place_ref[2] + dy, 2) * 4 + lax.rem(place_ref[3] + dz, 4)
            copy = pltpu.make_async_copy(
                block_ref.at[index],
                out_ref.at[pl.ds(pl.multiple_of(row * BLOCK, BLOCK), BLOCK), :],
                sems.at[index],
            )
            copy.start()
            copies.append(copy)
    for copy in copies:
        copy.wait()


def write_out(place, pieces, after):
    return pl.pallas_call(
        write_kernel,
        out_shape=[shape((LANES, TAPS * CH), F32), shape((8, LANES), F32)],
        in_specs=[smem()] + [vmem()] * 5 + [anywhere()],
        out_specs=[in_hbm(), vmem()],
        scratch_shapes=[
            pltpu.VMEM((8, BLOCK, TAPS * CH), F32),
            pltpu.SemaphoreType.DMA((8,)),
        ],
        compiler_params=params(),
        cost_estimate=cost(0, 6000000),
    )(place, *pieces, after)


def plus(*terms):
    total = terms[0].astype(F32)
    for term in terms[1:]:
        total = total + term.astype(F32)
    return total.astype(BF16)


def step_call(body, inputs, outputs, after=()):
    count = len(inputs)

    def kernel(*refs):
        body(refs[:count], refs[count + len(after) :])

    return pl.pallas_call(
        kernel,
        out_shape=[shape(dims) for dims in outputs],
        in_specs=[vmem()] * count + [anywhere()] * len(after),
        out_specs=[vmem()] * len(outputs),
        compiler_params=params(),
        cost_estimate=cost(0, 1500000),
    )(*inputs, *after)


WHOLE = (4, ROWS, LANES)
SINGLE = (ROWS, LANES)
FIRST_PART = (4, FIRST, LANES)
LAST_PART = (4, LAST, LANES)


def meet(ins, outs):
    y_first, x_in, x_last, y_in = ins
    outs[0][...] = plus(y_first[...], x_in[:, :FIRST])
    outs[1][...] = plus(x_last[...], y_in[:, :LAST])


def sum_quads(ins, outs):
    keep, x_in, x_last, y_first, y_in = ins
    for index, out in enumerate(outs):
        out[:FIRST] = plus(keep[index, :FIRST], x_in[index, FIRST:], y_first[index])
        out[FIRST:] = plus(keep[index, FIRST:], x_last[index], y_in[index, LAST:])


def sum_z(ins, outs):
    outs[0][...] = plus(*[ref[...] for ref in ins])


def stack_z(ins, outs):
    for index, ref in enumerate(ins):
        outs[0][index] = ref[...]


def cut_far(ins, outs):
    outs[0][...] = ins[0][:, :FIRST]
    outs[1][...] = ins[1][:, FIRST:]


def hand_on(ins, outs):
    for source, goal in zip(ins, outs):
        goal[...] = source[...]


def both(one, one_in, one_out, two):
    def body(ins, outs):
        one(ins[:one_in], outs[:one_out])
        two(ins[one_in:], outs[one_out:])

    return body


def reduce_diagonal(x_both, y_both):
    return shifted(x_both, "x", 1), shifted(y_both, "y", 1)


def reduce_sides(y_first, x_last):
    return shifted(y_first, "y", 1), shifted(x_last, "x", 1)


def reduce_z(rows):
    return [rows[0]] + [shifted(rows[by], "z", by) for by in range(1, 4)]


def gather_z(own):
    return [own] + [shifted(own, "z", -by) for by in range(1, 4)]


def gather_sides(whole):
    return whole, shifted(whole, "x", 1), shifted(whole, "y", 1)


def gather_diagonal(first, last):
    return shifted(first, "y", 1), shifted(last, "x", 1)


def any_reduce_gather(pieces, place):
    extents, _ = az_places(lax.axis_size("az"))
    count = lax.axis_size("az")
    keep, y_first, x_last, x_both, y_both = pieces
    join = lambda first, last: jnp.concatenate([first, last], axis=1)
    cut = jnp.stack(
        [
            keep,
            join(y_first, y_both[:, LAST:]),
            join(x_both[:, FIRST:], x_last),
            join(x_both[:, :FIRST], y_both[:, :LAST]),
        ]
    )
    order = ("x", "y", "z")
    full = cut.shape
    cut = cut.reshape([extents[name] for name in order] + [-1, LANES])
    for position, name in enumerate(order):
        cut = jnp.roll(cut, -place[name], axis=position)
    for name in order:
        cut = plus(cut[0], *[shifted(cut[by], name, by) for by in range(1, extents[name])])
    for name in order[::-1]:
        mine = cut
        cut = jnp.stack([mine] + [shifted(mine, name, -by) for by in range(1, extents[name])])
    for position, name in enumerate(order):
        cut = jnp.roll(cut, place[name], axis=position)
    cut = cut.reshape(full)
    return cut[0], cut[2], cut[1], cut[3][:, :FIRST], cut[3][:, FIRST:]


def local(features, cotangent, w_first, w_second):
    groups = lax.axis_size("grp")
    cells = lax.axis_size("az") * LAYERS * HALF * groups
    factor = 1.0 / math.sqrt(cells)
    extents, _ = az_places(lax.axis_size("az"))
    quad = extents == {"x": 2, "y": 2, "z": 4}
    spot = my_place()
    own = lax.axis_index("grp")
    zero = jnp.zeros((), jnp.int32)
    place = jnp.stack(
        [own] + [spot[name] if quad else zero for name in ("x", "y", "z")]
    ).astype(jnp.int32)

    f = features.transpose(1, 2, 0)
    c = cotangent.transpose(1, 2, 0)
    fc, to_next, to_last = pack(f, c)
    swap = neighbour(fc, 0, 1)
    up = neighbour(to_next, 1, 0)
    down = neighbour(to_last, -1, 0)
    w_one, w_two = load(w_first, w_second, to_last)
    halos = [up, neighbour(up, 0, 1), down, neighbour(down, 0, 1)]
    x, cot, send, back, slope = fields(place, fc, swap, halos, w_one, w_two)
    got = neighbour(send, 0, 1)
    hidden, second = second_grad(place, factor, cot, send, got)
    mine, theirs = flow(place, x, hidden, w_two)
    theirs = neighbour(theirs, 0, 1)
    if quad:
        corner = reduce_diagonal(*second[3:])
        first = first_grad(place, factor, back, got, slope, x, mine)
        sides = reduce_sides(
            *step_call(
                meet,
                [second[1], corner[0], second[2], corner[1]],
                [FIRST_PART, LAST_PART],
                [mine],
            )
        )
        *rows, x_both, y_both = step_call(
            both(sum_quads, 5, 4, hand_on),
            [second[0], corner[0], sides[1], sides[0], corner[1], first[3], first[4]],
            [SINGLE] * 4 + [first[3].shape, first[4].shape],
        )
        corner_two = reduce_diagonal(x_both, y_both)
        rows = reduce_z(rows)
        flow_out, token = join_flow(place, mine, theirs)
        own_one, *sides_two = step_call(
            both(sum_z, 4, 1, meet),
            [*rows, first[1], corner_two[0], first[2], corner_two[1]],
            [SINGLE, FIRST_PART, LAST_PART],
            [token],
        )
        sides_two = reduce_sides(*sides_two)
        blocks = gather_z(own_one)
        whole, *rows_two = step_call(
            both(stack_z, 4, 1, sum_quads),
            [*blocks, first[0], corner_two[0], sides_two[1], sides_two[0], corner_two[1]],
            [WHOLE] + [SINGLE] * 4,
        )
        near = gather_sides(whole)
        rows_two = reduce_z(rows_two)
        relay_first, relay_last, own_two = step_call(
            both(cut_far, 2, 2, sum_z),
            [near[1], near[2], *rows_two],
            [FIRST_PART, LAST_PART, SINGLE],
        )
        far = gather_diagonal(relay_first, relay_last)
        blocks_two = gather_z(own_two)
        (whole_two,) = step_call(stack_z, blocks_two, [WHOLE], far)
        near_two = gather_sides(whole_two)
        far_two = gather_diagonal(
            *step_call(cut_far, [near_two[1], near_two[2]], [FIRST_PART, LAST_PART])
        )
        grad_second, token = write_out(place, (*near, *far), whole_two)
        grad_first, _ = write_out(place, (*near_two, *far_two), token)
    else:
        flow_out, _ = join_flow(place, mine, theirs)
        first = first_grad(place, factor, back, got, slope, x, mine)
        grad_second, step = write_out(place, any_reduce_gather(second, spot), mine)
        grad_first, _ = write_out(place, any_reduce_gather(first, spot), step)
    return (flow_out.transpose(2, 0, 1), grad_first, grad_second)


def solution(mesh):
    in_specs = (P(None, "az", "grp"), P(None, "az", "grp"), P("grp", None), P("grp", None))
    out_specs = (P(None, "az", "grp"), P("grp", None), P("grp", None))
    return jax.shard_map(local, mesh=mesh, in_specs=in_specs, out_specs=out_specs, check_vma=False)
```

```python
import functools
import math

import jax
import jax.numpy as jnp
from jax import lax
from jax.experimental import pallas as pl
from jax.experimental.pallas import tpu as pltpu
from jax.sharding import PartitionSpec as P

AXIAL = 8
NRZ = 128
HALF = 64
LANES = 128
CH = 256
LAYERS = 4
TAPS = 27
BLOCK = 16
FIRST_TAPS = 14
ROWS = TAPS * BLOCK
FIRST = FIRST_TAPS * BLOCK
LAST = ROWS - FIRST
VMEM_LIMIT = 40 * 1024 * 1024
BF16 = jnp.bfloat16
F32 = jnp.float32


def params():
    return pltpu.CompilerParams(vmem_limit_bytes=VMEM_LIMIT)


def vmem():
    return pl.BlockSpec(memory_space=pltpu.VMEM)


def anywhere():
    return pl.BlockSpec(memory_space=pl.ANY)


def in_hbm():
    return pl.BlockSpec(memory_space=pltpu.HBM)


def smem():
    return pl.BlockSpec(memory_space=pltpu.SMEM)


def shape(dims, kind=BF16):
    return jax.ShapeDtypeStruct(dims, kind)


def cost(flops, moved):
    return pl.CostEstimate(flops=flops, bytes_accessed=moved, transcendentals=0)


def az_extents(count):
    side = 1
    while (2 * side) ** 3 <= count:
        side *= 2
    if count % (side * side):
        side = 1
    return {"z": count // (side * side), "y": side, "x": side}


def az_places(count):
    extents = az_extents(count)
    places = []
    for index in range(count):
        rest, x = divmod(index, extents["x"])
        z, y = divmod(rest, extents["y"])
        places.append({"z": z, "y": y, "x": x})
    return extents, places


def shifted(value, along, by):
    extents, places = az_places(lax.axis_size("az"))
    pairs = []
    for index, place in enumerate(places):
        goal = dict(place)
        goal[along] = (place[along] + by) % extents[along]
        pairs.append((index, (goal["z"] * extents["y"] + goal["y"]) * extents["x"] + goal["x"]))
    return lax.ppermute(value, "az", pairs)


def my_place():
    extents, _ = az_places(lax.axis_size("az"))
    me = lax.axis_index("az")
    x = me % extents["x"]
    y = (me // extents["x"]) % extents["y"]
    z = me // (extents["x"] * extents["y"])
    return {"z": z, "y": y, "x": x}


def neighbour(value, az_by, grp_by):
    count = lax.axis_size("az")
    groups = lax.axis_size("grp")
    pairs = []
    for a in range(count):
        for g in range(groups):
            goal = ((a + az_by) % count) * groups + (g + grp_by) % groups
            pairs.append((a * groups + g, goal))
    return lax.ppermute(value, ("az", "grp"), pairs)


def tap_slice(ref, tap):
    return ref[:, tap * CH : (tap + 1) * CH]


def roll_rows(value, by):
    count = value.shape[0]
    rolled = pltpu.roll(value, by % count, axis=0)
    z = lax.broadcasted_iota(jnp.int32, value.shape, 0) % AXIAL
    edge = 0 if by == 1 else AXIAL - 1
    return jnp.where(z == edge, 0.0, rolled)


def shift_radius(value, by):
    layers, _, lanes = value.shape
    empty = jnp.zeros((layers, AXIAL, lanes), value.dtype)
    if by == 1:
        return jnp.concatenate([empty, value[:, : NRZ - AXIAL]], axis=1)
    return jnp.concatenate([value[:, AXIAL:], empty], axis=1)


def forward_weights(w_ref, s, p):
    return jnp.concatenate([tap_slice(w_ref, (p * 3 + q) * 3 + s) for q in range(3)], axis=0)


def dot_rows(lhs, rhs):
    return lax.dot_general(lhs, rhs, (((1,), (1,)), ((), ())), preferred_element_type=F32)


def fold_forward(part, s):
    layers = part.shape[0]
    summed = part[:, :, LANES : 2 * LANES]
    summed = summed + shift_radius(part[:, :, :LANES], 1)
    summed = summed + shift_radius(part[:, :, 2 * LANES :], -1)
    summed = summed.reshape(layers * NRZ, LANES)
    return summed if s == 1 else roll_rows(summed, 1 - s)


def conv_rows(x_ref, w_ref, layers, first):
    count = layers * NRZ
    lhs = jnp.concatenate(
        [x_ref[(first + p) * NRZ : (first + p) * NRZ + count, :] for p in range(3)], axis=1
    )
    total = None
    for s in range(3):
        rhs = jnp.concatenate([forward_weights(w_ref, s, p) for p in range(3)], axis=1)
        part = fold_forward(dot_rows(lhs, rhs).reshape(layers, NRZ, 3 * LANES), s)
        total = part if total is None else total + part
    return total


def pick_half(value, own):
    low = value[..., :LANES].astype(F32)
    high = value[..., LANES:].astype(F32)
    return jnp.where(jnp.broadcast_to(own, low.shape) == 0, low, high)


def pack_kernel(f_ref, c_ref, fc_ref, next_ref, last_ref, sems):
    copies = [
        (f_ref, fc_ref.at[:LAYERS]),
        (c_ref, fc_ref.at[LAYERS:]),
        (f_ref.at[LAYERS - 2 :], next_ref.at[:2]),
        (c_ref.at[LAYERS - 1 :], next_ref.at[2:]),
        (f_ref.at[:2], last_ref.at[:2]),
        (c_ref.at[:1], last_ref.at[2:]),
    ]
    copies = [pltpu.make_async_copy(a, b, sems.at[i]) for i, (a, b) in enumerate(copies)]
    for copy in copies:
        copy.start()
    for copy in copies:
        copy.wait()


def pack(f, c):
    return pl.pallas_call(
        pack_kernel,
        out_shape=[
            shape((2 * LAYERS, HALF, CH)),
            shape((3, HALF, CH)),
            shape((3, HALF, CH)),
        ],
        in_specs=[in_hbm()] * 2,
        out_specs=[vmem()] * 3,
        scratch_shapes=[pltpu.SemaphoreType.DMA((6,))],
        compiler_params=params(),
        cost_estimate=cost(0, 900000),
    )(f, c)


def inner_kernel(
    place_ref, fc_ref, swap_ref, w1_ref, w2_ref, x_ref, cot_ref, pre_ref, back_ref, acc_ref
):
    own = place_ref[0]
    mine = pl.multiple_of(own * HALF, HALF)
    other = pl.multiple_of((1 - own) * HALF, HALF)
    for layer in range(LAYERS):
        x_ref[pl.ds(layer * NRZ + mine, HALF), :] = fc_ref[layer]
        x_ref[pl.ds(layer * NRZ + other, HALF), :] = swap_ref[layer]
        cot_ref[pl.ds(layer * NRZ + mine, HALF), :] = pick_half(
            fc_ref[LAYERS + layer], own
        ).astype(BF16)
        cot_ref[pl.ds(layer * NRZ + other, HALF), :] = pick_half(
            swap_ref[LAYERS + layer], own
        ).astype(BF16)

    count = LAYERS * NRZ
    total = None
    for s in range(3):
        acc_ref[...] = jnp.zeros_like(acc_ref)
        for p in range(3):
            rows = slice((2 - p) * NRZ, (2 - p) * NRZ + count)
            acc_ref[rows, :] += dot_rows(x_ref[...], forward_weights(w1_ref, s, p))
        part = fold_forward(acc_ref[...].reshape(LAYERS + 2, NRZ, 3 * LANES), s)
        total = part if total is None else total + part
    pre_ref[...] = total

    empty = jnp.zeros((NRZ, LANES), BF16)
    lhs = jnp.concatenate(
        [
            jnp.concatenate([cot_ref[NRZ:, :], empty], axis=0),
            cot_ref[...],
            jnp.concatenate([empty, cot_ref[: count - NRZ, :]], axis=0),
        ],
        axis=1,
    )
    total = None
    for s in range(3):
        summed = None
        for q in range(3):
            rhs = jnp.concatenate(
                [tap_slice(w2_ref, (p * 3 + q) * 3 + s) for p in range(3)], axis=0
            )
            part = jnp.dot(lhs, rhs, preferred_element_type=F32).reshape(LAYERS, NRZ, CH)
            if q != 1:
                part = shift_radius(part, q - 1)
            summed = part if summed is None else summed + part
        summed = summed.reshape(count, CH)
        if s != 1:
            summed = roll_rows(summed, s - 1)
        total = summed if total is None else total + summed
    back_ref[...] = total


def inner(place, fc, swap, w_first, w_second):
    return pl.pallas_call(
        inner_kernel,
        out_shape=[
            shape((LAYERS * NRZ, CH)),
            shape((LAYERS * NRZ, LANES)),
            shape(((LAYERS + 2) * NRZ, LANES), F32),
            shape((LAYERS * NRZ, CH), F32),
        ],
        in_specs=[smem()] + [vmem()] * 4,
        out_specs=[vmem()] * 4,
        scratch_shapes=[pltpu.VMEM(((LAYERS + 2) * NRZ, 3 * LANES), F32)],
        compiler_params=params(),
        cost_estimate=cost(2300000000, 6000000),
    )(place, fc, swap, w_first, w_second)


def fields_kernel(
    place_ref, x_in, cot_in, pre_in, back_in, same_ref, cross_ref,
    w1_ref, w2_ref, x_ref, cot_ref, send_ref, back_ref, slope_ref, sum_ref,
):
    own = place_ref[0]
    mine = pl.multiple_of(own * HALF, HALF)
    other = pl.multiple_of((1 - own) * HALF, HALF)
    up_same, down_same = same_ref.at[:3], same_ref.at[3:]
    up_cross, down_cross = cross_ref.at[:3], cross_ref.at[3:]
    for layer in range(2):
        x_ref[pl.ds(layer * NRZ + mine, HALF), :] = up_same[layer]
        x_ref[pl.ds(layer * NRZ + other, HALF), :] = up_cross[layer]
        x_ref[pl.ds((6 + layer) * NRZ + mine, HALF), :] = down_same[layer]
        x_ref[pl.ds((6 + layer) * NRZ + other, HALF), :] = down_cross[layer]
    x_ref[2 * NRZ : 6 * NRZ, :] = x_in[...]
    cot_ref[NRZ : 5 * NRZ, :] = cot_in[...]
    cot_ref[pl.ds(mine, HALF), :] = pick_half(up_same[2], own).astype(BF16)
    cot_ref[pl.ds(other, HALF), :] = pick_half(up_cross[2], own).astype(BF16)
    cot_ref[pl.ds(5 * NRZ + mine, HALF), :] = pick_half(down_same[2], own).astype(BF16)
    cot_ref[pl.ds(5 * NRZ + other, HALF), :] = pick_half(down_cross[2], own).astype(BF16)

    low = x_ref[: 2 * NRZ, :]
    high = x_ref[6 * NRZ :, :]
    middle = jnp.concatenate([x_ref[NRZ : 2 * NRZ, :], x_ref[6 * NRZ : 7 * NRZ, :]], axis=0)
    edge = None
    for s in range(3):
        zero = dot_rows(low, forward_weights(w1_ref, s, 0))
        one = dot_rows(middle, forward_weights(w1_ref, s, 1))
        two = dot_rows(high, forward_weights(w1_ref, s, 2))
        part = jnp.concatenate(
            [zero[:NRZ] + one[:NRZ], zero[NRZ:], two[:NRZ], one[NRZ:] + two[NRZ:]], axis=0
        )
        part = fold_forward(part.reshape(4, NRZ, 3 * LANES), s)
        edge = part if edge is None else edge + part
    sum_ref[...] = pre_in[...]
    sum_ref[: 2 * NRZ, :] += edge[: 2 * NRZ]
    sum_ref[4 * NRZ :, :] += edge[2 * NRZ :]
    pre = sum_ref[...]
    sigma = jax.nn.sigmoid(pre)
    send_ref[: (LAYERS + 2) * NRZ, :] = (pre * sigma).astype(BF16)
    within = pre[NRZ : NRZ * (LAYERS + 1)]
    sigma = sigma[NRZ : NRZ * (LAYERS + 1)]
    slope_ref[...] = sigma * (1.0 + within * (1.0 - sigma))

    first = cot_ref[:NRZ, :]
    last = cot_ref[5 * NRZ :, :]
    edge = None
    for s in range(3):
        summed = None
        for q in range(3):
            part = jnp.concatenate(
                [
                    jnp.dot(first, tap_slice(w2_ref, (6 + q) * 3 + s), preferred_element_type=F32),
                    jnp.dot(last, tap_slice(w2_ref, q * 3 + s), preferred_element_type=F32),
                ],
                axis=0,
            ).reshape(2, NRZ, CH)
            if q != 1:
                part = shift_radius(part, q - 1)
            summed = part if summed is None else summed + part
        summed = summed.reshape(2 * NRZ, CH)
        if s != 1:
            summed = roll_rows(summed, s - 1)
        edge = summed if edge is None else edge + summed
    rows = LAYERS * NRZ
    total = jnp.concatenate(
        [
            back_in[:NRZ, :] + edge[:NRZ],
            back_in[NRZ : rows - NRZ, :],
            back_in[rows - NRZ :, :] + edge[NRZ:],
        ],
        axis=0,
    )
    back_ref[...] = pick_half(total, own)
    send_ref[(LAYERS + 2) * NRZ :, :] = pick_half(total, 1 - own).astype(BF16)


def fields(place, own_parts, halos, w_first, w_second):
    rows = (LAYERS + 2) * NRZ
    return pl.pallas_call(
        fields_kernel,
        out_shape=[
            shape(((LAYERS + 4) * NRZ, CH)),
            shape((rows, LANES)),
            shape((rows + LAYERS * NRZ, LANES)),
            shape((LAYERS * NRZ, LANES), F32),
            shape((LAYERS * NRZ, LANES), F32),
        ],
        in_specs=[smem()] + [vmem()] * 8,
        out_specs=[vmem()] * 5,
        scratch_shapes=[pltpu.VMEM((rows, LANES), F32)],
        compiler_params=params(),
        cost_estimate=cost(1000000000, 6000000),
    )(place, *own_parts, *halos, w_first, w_second)


def grad_pieces(place_ref, source, field, factor, turned_ref, outs):
    own_x = place_ref[1]
    own_y = place_ref[2]
    own_z = place_ref[3]
    keep, y_first, x_last, x_both, y_both = outs
    lane = lax.broadcasted_iota(jnp.int32, (LANES, NRZ), 1)
    z = lane % AXIAL
    r = lane // AXIAL
    for layer in range(LAYERS):
        turned = source[layer * NRZ : (layer + 1) * NRZ, :].T
        for q in range(3):
            for s in range(3):
                by = AXIAL * (q - 1) + (s - 1)
                moved = pltpu.roll(turned, by % NRZ, axis=1) if by else turned
                if q == 0:
                    moved = jnp.where(r == NRZ // AXIAL - 1, 0.0, moved)
                if q == 2:
                    moved = jnp.where(r == 0, 0.0, moved)
                if s == 0:
                    moved = jnp.where(z == AXIAL - 1, 0.0, moved)
                if s == 2:
                    moved = jnp.where(z == 0, 0.0, moved)
                row = (q * 3 + s) * LANES
                turned_ref[row : row + LANES, layer * NRZ : (layer + 1) * NRZ] = moved.astype(BF16)
    x_zero = jnp.broadcast_to(own_x, (LANES, LANES)) == 0
    y_zero = jnp.broadcast_to(own_y, (HALF, LANES)) == 0
    slots = [lax.rem(index - own_z + 4, 4) for index in range(4)]
    for p in range(3):
        product = jnp.dot(turned_ref[...], field(p), preferred_element_type=F32) * factor
        for within in range(9):
            tap = p * 9 + within
            value = product[within * LANES : (within + 1) * LANES]
            low = value[:, :LANES]
            high = value[:, LANES:]
            halves = (jnp.where(x_zero, low, high), jnp.where(x_zero, high, low))
            for dx in range(2):
                top = halves[dx][:HALF]
                bottom = halves[dx][HALF:]
                parts = (jnp.where(y_zero, top, bottom), jnp.where(y_zero, bottom, top))
                for dy in range(2):
                    early = tap < FIRST_TAPS
                    row = (tap if early else tap - FIRST_TAPS) * BLOCK
                    if dx == 0 and dy == 0:
                        ref, row = keep, tap * BLOCK
                    elif dx == 1 and dy == 1:
                        ref = x_both if early else y_both
                    elif dx == 1:
                        ref, row = (x_both, FIRST + row) if early else (x_last, row)
                    else:
                        ref, row = (y_first, row) if early else (y_both, LAST + row)
                    narrow = parts[dy].astype(BF16)
                    for index in range(4):
                        ref[slots[index], row : row + BLOCK, :] = narrow[
                            index * BLOCK : (index + 1) * BLOCK
                        ]


def second_kernel(factor, place_ref, cot_ref, send_ref, got_ref, h_ref, *rest):
    outs, turned_ref = rest[:5], rest[5]
    rows = (LAYERS + 2) * NRZ
    own = place_ref[0]
    mine = send_ref[:rows, :].astype(F32)
    other = got_ref[:rows, :].astype(F32)
    first = jnp.broadcast_to(own, mine.shape) == 0
    h_ref[:, :LANES] = jnp.where(first, mine, other).astype(BF16)
    h_ref[:, LANES:] = jnp.where(first, other, mine).astype(BF16)
    source = cot_ref[NRZ : NRZ * (LAYERS + 1), :].astype(F32)
    field = lambda p: h_ref[p * NRZ : p * NRZ + LAYERS * NRZ, :]
    grad_pieces(place_ref, source, field, factor, turned_ref, outs)


def first_kernel(factor, place_ref, back_ref, got_ref, slope_ref, x_ref, after, *rest):
    outs, turned_ref = rest[:5], rest[5]
    rows = (LAYERS + 2) * NRZ
    source = (back_ref[...] + got_ref[rows:, :].astype(F32)) * slope_ref[...]
    source = source.astype(BF16).astype(F32)
    field = lambda p: x_ref[(p + 1) * NRZ : (p + 1) * NRZ + LAYERS * NRZ, :]
    grad_pieces(place_ref, source, field, factor, turned_ref, outs)


def piece_shapes():
    return [shape((4, rows, LANES)) for rows in (ROWS, FIRST, LAST, 2 * FIRST, 2 * LAST)]


def second_grad(place, factor, cot, send, got):
    outs = pl.pallas_call(
        functools.partial(second_kernel, factor),
        out_shape=[shape(((LAYERS + 2) * NRZ, CH))] + piece_shapes(),
        in_specs=[smem()] + [vmem()] * 3,
        out_specs=[vmem()] * 6,
        scratch_shapes=[pltpu.VMEM((9 * LANES, LAYERS * NRZ), BF16)],
        compiler_params=params(),
        cost_estimate=cost(1000000000, 3000000),
    )(place, cot, send, got)
    return outs[0], outs[1:]


def first_grad(place, factor, back, got, slope, x, after):
    return pl.pallas_call(
        functools.partial(first_kernel, factor),
        out_shape=piece_shapes(),
        in_specs=[smem()] + [vmem()] * 4 + [anywhere()],
        out_specs=[vmem()] * 5,
        scratch_shapes=[pltpu.VMEM((9 * LANES, LAYERS * NRZ), BF16)],
        compiler_params=params(),
        cost_estimate=cost(1000000000, 3000000),
    )(place, back, got, slope, x, after)


def flow_kernel(place_ref, x_ref, h_ref, w2_ref, keep_ref, send_ref):
    own = place_ref[0]
    result = conv_rows(h_ref, w2_ref, LAYERS, 0)
    result = result + pick_half(x_ref[2 * NRZ : 2 * NRZ + LAYERS * NRZ, :], own)
    halves = result.reshape(LAYERS, 2, HALF, LANES)
    first = jnp.broadcast_to(own, (LAYERS, HALF, LANES)) == 0
    keep_ref[...] = jnp.where(first, halves[:, 0], halves[:, 1]).astype(BF16)
    send_ref[...] = jnp.where(first, halves[:, 1], halves[:, 0]).astype(BF16)


def flow(place, x, h, w_second):
    return pl.pallas_call(
        flow_kernel,
        out_shape=[shape((LAYERS, HALF, LANES))] * 2,
        in_specs=[smem()] + [vmem()] * 3,
        out_specs=[vmem()] * 2,
        compiler_params=params(),
        cost_estimate=cost(1000000000, 3000000),
    )(place, x, h, w_second)


def join_kernel(place_ref, mine_ref, theirs_ref, out_ref, token_ref):
    token_ref[...] = jnp.zeros_like(token_ref)
    mine = mine_ref[...].astype(F32)
    theirs = theirs_ref[...].astype(F32)
    first = jnp.broadcast_to(place_ref[0], mine.shape) == 0
    out_ref[:, :, :LANES] = jnp.where(first, mine, theirs).astype(BF16)
    out_ref[:, :, LANES:] = jnp.where(first, theirs, mine).astype(BF16)


def join_flow(place, mine, theirs):
    return pl.pallas_call(
        join_kernel,
        out_shape=[shape((LAYERS, HALF, CH)), shape((8, LANES), F32)],
        in_specs=[smem()] + [vmem()] * 2,
        out_specs=[vmem()] * 2,
        compiler_params=params(),
        cost_estimate=cost(0, 400000),
    )(place, mine, theirs)


def write_half(far, place_ref, near_ref, across_refs, out_ref, block_ref, sems):
    x_zero = jnp.broadcast_to(place_ref[1], (BLOCK, LANES)) == 0
    copies = []
    for dz in range(4):
        for tap in range(TAPS):
            rows = slice(tap * BLOCK, (tap + 1) * BLOCK)
            near = near_ref[dz, rows, :].astype(F32)
            if len(across_refs) == 1:
                across = across_refs[0][dz, rows, :]
            elif tap < FIRST_TAPS:
                across = across_refs[0][dz, rows, :]
            else:
                late = slice((tap - FIRST_TAPS) * BLOCK, (tap - FIRST_TAPS + 1) * BLOCK)
                across = across_refs[1][dz, late, :]
            across = across.astype(F32)
            lanes = slice(tap * CH, tap * CH + LANES)
            block_ref[dz, :, lanes] = jnp.where(x_zero, near, across)
            lanes = slice(tap * CH + LANES, (tap + 1) * CH)
            block_ref[dz, :, lanes] = jnp.where(x_zero, across, near)
        row = lax.rem(place_ref[2] + far, 2) * 4 + lax.rem(place_ref[3] + dz, 4)
        copy = pltpu.make_async_copy(
            block_ref.at[dz],
            out_ref.at[pl.ds(pl.multiple_of(row * BLOCK, BLOCK), BLOCK), :],
            sems.at[dz],
        )
        copy.start()
        copies.append(copy)
    for copy in copies:
        copy.wait()


def write_near_kernel(place_ref, m_ref, mx_ref, after, out_ref, token_ref, block_ref, sems):
    token_ref[...] = jnp.zeros_like(token_ref)
    write_half(0, place_ref, m_ref, [mx_ref], out_ref, block_ref, sems)


def write_far_kernel(
    place_ref, my_ref, first_ref, last_ref, half_ref, out_ref, token_ref, block_ref, sems
):
    token_ref[...] = jnp.zeros_like(token_ref)
    write_half(1, place_ref, my_ref, [first_ref, last_ref], out_ref, block_ref, sems)


def write_shapes():
    return {
        "out_shape": [shape((LANES, TAPS * CH), F32), shape((8, LANES), F32)],
        "out_specs": [in_hbm(), vmem()],
        "scratch_shapes": [
            pltpu.VMEM((4, BLOCK, TAPS * CH), F32),
            pltpu.SemaphoreType.DMA((4,)),
        ],
        "compiler_params": params(),
        "cost_estimate": cost(0, 3000000),
    }


def write_near(place, whole, across_x, after):
    return pl.pallas_call(
        write_near_kernel,
        in_specs=[smem()] + [vmem()] * 2 + [anywhere()],
        **write_shapes(),
    )(place, whole, across_x, after)


def write_far(place, across_y, first, last, half):
    return pl.pallas_call(
        write_far_kernel,
        in_specs=[smem()] + [vmem()] * 3 + [in_hbm()],
        input_output_aliases={4: 0},
        **write_shapes(),
    )(place, across_y, first, last, half)


def write_out(place, pieces, after):
    whole, across_x, across_y, first, last = pieces
    half, _ = write_near(place, whole, across_x, after)
    return write_far(place, across_y, first, last, half)


def plus(*terms):
    total = terms[0].astype(F32)
    for term in terms[1:]:
        total = total + term.astype(F32)
    return total.astype(BF16)


def step_call(body, inputs, outputs, after=()):
    count = len(inputs)

    def kernel(*refs):
        body(refs[:count], refs[count + len(after) :])

    return pl.pallas_call(
        kernel,
        out_shape=[shape(dims) for dims in outputs],
        in_specs=[vmem()] * count + [anywhere()] * len(after),
        out_specs=[vmem()] * len(outputs),
        compiler_params=params(),
        cost_estimate=cost(0, 1500000),
    )(*inputs, *after)


WHOLE = (4, ROWS, LANES)
SINGLE = (ROWS, LANES)
FIRST_PART = (4, FIRST, LANES)
LAST_PART = (4, LAST, LANES)


def meet(ins, outs):
    y_first, x_in, x_last, y_in = ins
    outs[0][...] = plus(y_first[...], x_in[:, :FIRST])
    outs[1][...] = plus(x_last[...], y_in[:, :LAST])


def sum_quads(ins, outs):
    keep, x_in, x_last, y_first, y_in = ins
    for index, out in enumerate(outs):
        out[:FIRST] = plus(keep[index, :FIRST], x_in[index, FIRST:], y_first[index])
        out[FIRST:] = plus(keep[index, FIRST:], x_last[index], y_in[index, LAST:])


def sum_z(ins, outs):
    outs[0][...] = plus(*[ref[...] for ref in ins])


def stack_z(ins, outs):
    for index, ref in enumerate(ins):
        outs[0][index] = ref[...]


def cut_far(ins, outs):
    outs[0][...] = ins[0][:, :FIRST]
    outs[1][...] = ins[1][:, FIRST:]


def hand_on(ins, outs):
    for source, goal in zip(ins, outs):
        goal[...] = source[...]


def both(one, one_in, one_out, two):
    def body(ins, outs):
        one(ins[:one_in], outs[:one_out])
        two(ins[one_in:], outs[one_out:])

    return body


def join_halos(ins, outs):
    outs[0][:3] = ins[0][...]
    outs[0][3:] = ins[1][...]


def reduce_diagonal(x_both, y_both):
    return shifted(x_both, "x", 1), shifted(y_both, "y", 1)


def reduce_sides(y_first, x_last):
    return shifted(y_first, "y", 1), shifted(x_last, "x", 1)


def reduce_z(rows):
    return [rows[0]] + [shifted(rows[by], "z", by) for by in range(1, 4)]


def gather_z(own):
    return [own] + [shifted(own, "z", -by) for by in range(1, 4)]


def gather_sides(whole):
    return whole, shifted(whole, "x", 1), shifted(whole, "y", 1)


def gather_diagonal(first, last):
    return shifted(first, "y", 1), shifted(last, "x", 1)


def any_reduce_gather(pieces, place):
    extents, _ = az_places(lax.axis_size("az"))
    count = lax.axis_size("az")
    keep, y_first, x_last, x_both, y_both = pieces
    join = lambda first, last: jnp.concatenate([first, last], axis=1)
    cut = jnp.stack(
        [
            keep,
            join(y_first, y_both[:, LAST:]),
            join(x_both[:, FIRST:], x_last),
            join(x_both[:, :FIRST], y_both[:, :LAST]),
        ]
    )
    order = ("x", "y", "z")
    full = cut.shape
    cut = cut.reshape([extents[name] for name in order] + [-1, LANES])
    for position, name in enumerate(order):
        cut = jnp.roll(cut, -place[name], axis=position)
    for name in order:
        cut = plus(cut[0], *[shifted(cut[by], name, by) for by in range(1, extents[name])])
    for name in order[::-1]:
        mine = cut
        cut = jnp.stack([mine] + [shifted(mine, name, -by) for by in range(1, extents[name])])
    for position, name in enumerate(order):
        cut = jnp.roll(cut, place[name], axis=position)
    cut = cut.reshape(full)
    return cut[0], cut[2], cut[1], cut[3][:, :FIRST], cut[3][:, FIRST:]


def local(features, cotangent, w_first, w_second):
    groups = lax.axis_size("grp")
    cells = lax.axis_size("az") * LAYERS * HALF * groups
    factor = 1.0 / math.sqrt(cells)
    extents, _ = az_places(lax.axis_size("az"))
    quad = extents == {"x": 2, "y": 2, "z": 4}
    spot = my_place()
    own = lax.axis_index("grp")
    zero = jnp.zeros((), jnp.int32)
    place = jnp.stack(
        [own] + [spot[name] if quad else zero for name in ("x", "y", "z")]
    ).astype(jnp.int32)

    f = features.transpose(1, 2, 0)
    c = cotangent.transpose(1, 2, 0)
    fc, to_next, to_last = pack(f, c)
    swap = neighbour(fc, 0, 1)
    up = neighbour(to_next, 1, 0)
    down = neighbour(to_last, -1, 0)
    own_parts = inner(place, fc, swap, w_first, w_second)
    (halos,) = step_call(join_halos, [up, down], [(6, HALF, CH)], [own_parts[2]])
    halos = [halos, neighbour(halos, 0, 1)]
    x, cot, send, back, slope = fields(place, own_parts, halos, w_first, w_second)
    got = neighbour(send, 0, 1)
    hidden, second = second_grad(place, factor, cot, send, got)
    mine, theirs = flow(place, x, hidden, w_second)
    theirs = neighbour(theirs, 0, 1)
    if quad:
        corner = reduce_diagonal(*second[3:])
        first = first_grad(place, factor, back, got, slope, x, mine)
        sides = reduce_sides(
            *step_call(
                meet,
                [second[1], corner[0], second[2], corner[1]],
                [FIRST_PART, LAST_PART],
                [mine],
            )
        )
        flow_out, token = join_flow(place, mine, theirs)
        *rows, x_both, y_both = step_call(
            both(sum_quads, 5, 4, hand_on),
            [second[0], corner[0], sides[1], sides[0], corner[1], first[3], first[4]],
            [SINGLE] * 4 + [first[3].shape, first[4].shape],
            [token],
        )
        corner_two = reduce_diagonal(x_both, y_both)
        rows = reduce_z(rows)
        own_one, *sides_two = step_call(
            both(sum_z, 4, 1, meet),
            [*rows, first[1], corner_two[0], first[2], corner_two[1]],
            [SINGLE, FIRST_PART, LAST_PART],
        )
        sides_two = reduce_sides(*sides_two)
        blocks = gather_z(own_one)
        whole, *rows_two = step_call(
            both(stack_z, 4, 1, sum_quads),
            [*blocks, first[0], corner_two[0], sides_two[1], sides_two[0], corner_two[1]],
            [WHOLE] + [SINGLE] * 4,
        )
        near = gather_sides(whole)
        rows_two = reduce_z(rows_two)
        relay_first, relay_last, own_two = step_call(
            both(cut_far, 2, 2, sum_z),
            [near[1], near[2], *rows_two],
            [FIRST_PART, LAST_PART, SINGLE],
        )
        far = gather_diagonal(relay_first, relay_last)
        blocks_two = gather_z(own_two)
        (whole_two,) = step_call(stack_z, blocks_two, [WHOLE], far)
        near_two = gather_sides(whole_two)
        grad_second, token = write_out(place, (*near, *far), whole_two)
        far_two = gather_diagonal(
            *step_call(cut_far, [near_two[1], near_two[2]], [FIRST_PART, LAST_PART], [token])
        )
        grad_first, _ = write_out(place, (*near_two, *far_two), token)
    else:
        flow_out, _ = join_flow(place, mine, theirs)
        first = first_grad(place, factor, back, got, slope, x, mine)
        grad_second, step = write_out(place, any_reduce_gather(second, spot), mine)
        grad_first, _ = write_out(place, any_reduce_gather(first, spot), step)
    return (flow_out.transpose(2, 0, 1), grad_first, grad_second)


def solution(mesh):
    in_specs = (P(None, "az", "grp"), P(None, "az", "grp"), P("grp", None), P("grp", None))
    out_specs = (P(None, "az", "grp"), P("grp", None), P("grp", None))
    return jax.shard_map(local, mesh=mesh, in_specs=in_specs, out_specs=out_specs, check_vma=False)
```
